256 devices in a mesh: node: 16 (over z, core), chip: 16 (over y, x).
Axes of the slice: x: 4, y: 4, z: 8, core: 2. Of those that a mesh axis runs over, the one named last changes fastest.
Arguments:
- x_rows: bfloat16 [49152, 12288], P(('node', 'chip')), may hold values from -6 to 6
- value_cot: bfloat16 [49152, 1024], P(('node', 'chip')), may hold values from -48 to 48
- value_weight: bfloat16 [12288, 1024], P('chip'), may hold values from -0.5 to 0.5
- resp_of_row: int32 [49152], P(('node', 'chip')), may hold values from 0 to 512, as said below
- block_plan: int32 [4096, 3], P(('node', 'chip')), may hold values from -1 to 15, as said below
- resp_len: int32 [512], replicated, may hold values from 1 to 143, as said below
- group_of_resp: int32 [512], replicated, may hold values from 0 to 63, as said below
- rewards: float32 [512], replicated, may hold values from -4 to 4
- send_error: bfloat16 [16, 12288, 1024], P('node', 'chip'), may hold values from -12 to 12
- mean_error: float32 [16, 16, 48, 1024], P('chip', 'node'), may hold values from -6 to 6
Outputs:
- input_grad: bfloat16 [36864, 12288], P(('node', 'chip'))
- new_send_error: bfloat16 [16, 12288, 1024], P('node', 'chip')
- new_mean_error: float32 [16, 16, 48, 1024], P('chip', 'node')
- update: bfloat16 [12288, 1024], P('chip')
The draws below stay inside these ranges and needn't reach their ends.
Inputs may be any that keep to these rules, and one draw needn't show every extreme that they name: `resp_of_row`: live rows come in whole blocks of 12; each response's rows are consecutive among the live rows of its replica taken in device order; 512 marks a padding row. A device holds between 8 and 16 live blocks. `block_plan`: A live block's receiving chip is in its own replica; every chip receives exactly 12 blocks, one for each place below 12; one device sends at most 1 block to one chip (its send slot is always 0), and some devices send exactly 1 to every chip. A padding block has -1 in all three entries. `resp_len`: the number of rows with that response. `group_of_resp`: every group holds exactly 8 responses.
All inputs are finite; a program needn't handle non-finite values. Where the reference program divides by a largest or mean magnitude, that divisor is 1e-20 or more.
Results may differ from the reference program's by a relative error of at most 0.012.
Values may be sent and summed in bfloat16 or wider, within the bound.
A program may use at most 128 MiB of HBM per device.

```python
import jax
import jax.numpy as jnp
from jax import lax

D = 12288
KV = 1024
BLK = 12
NBLK = 16
GSIZE = 8
LIVE = 12
ROWS = 144
TOKENS = 49152
NBLOCKS = 4096
PAIR = 1
RESP_NODE = 32
RESP = 512
GROUPS = 64
PIECE = 48
N_NODE = 16
N_CHIP = 16
DEVICES = 256


def layout(key):
    positions = jnp.arange(N_CHIP, dtype=jnp.int32)
    live_at = jnp.where(positions % 2 == 0, NBLK, NBLK // 2).astype(jnp.int32)
    node_keys = jax.random.split(jax.random.fold_in(key, 101), N_NODE)
    chip_order = jax.vmap(lambda one_key: jax.random.permutation(one_key, N_CHIP))(node_keys).astype(jnp.int32)
    node_index = jnp.arange(N_NODE, dtype=jnp.int32)[:, None]
    where_is = jnp.zeros((N_NODE, N_CHIP), jnp.int32).at[node_index, chip_order].set(jnp.broadcast_to(positions[None, :], (N_NODE, N_CHIP)))
    block_keys = jax.random.split(jax.random.fold_in(key, 102), N_NODE * N_CHIP)
    block_rank = jax.vmap(lambda one_key: jax.random.permutation(one_key, NBLK))(block_keys).astype(jnp.int32).reshape(N_NODE, N_CHIP, NBLK)
    own_spot = where_is[:, :, None]
    is_live = block_rank < live_at[where_is][:, :, None]
    dest_spot = (own_spot + block_rank) % N_CHIP
    dest_chip = jnp.take_along_axis(chip_order, dest_spot.reshape(N_NODE, N_CHIP * NBLK), axis=1).reshape(N_NODE, N_CHIP, NBLK)
    pair_slot = block_rank // N_CHIP
    offset_in = block_rank % N_CHIP
    spot_grid = positions[:, None, None]
    slot_grid = jnp.arange(PAIR, dtype=jnp.int32)[None, :, None]
    offset_grid = positions[None, None, :]
    incoming = (offset_grid + slot_grid * N_CHIP < live_at[(spot_grid - offset_grid) % N_CHIP]).astype(jnp.int32).reshape(N_CHIP, PAIR * N_CHIP)
    earlier = jnp.cumsum(incoming, axis=1) - incoming
    compact = earlier[dest_spot, pair_slot * N_CHIP + offset_in]
    plan = jnp.stack([dest_chip, pair_slot, compact], axis=-1)
    plan = jnp.where(is_live[..., None], plan, -1).astype(jnp.int32).reshape(NBLOCKS, 3)
    row_live = jnp.repeat(is_live.reshape(N_NODE, N_CHIP * NBLK), BLK, axis=1)
    live_rank = jnp.cumsum(row_live.astype(jnp.int32), axis=1) - 1
    live_total = N_CHIP * LIVE * BLK
    mean_len = live_total // RESP_NODE
    half_count = RESP_NODE // 2
    spread = jax.random.randint(jax.random.fold_in(key, 104), (N_NODE, half_count), 0, mean_len).astype(jnp.int32)
    spread = spread.at[:, 0].set(mean_len - 1)
    paired = jnp.concatenate([mean_len + spread, mean_len - spread], axis=1).astype(jnp.int32)
    order_keys = jax.random.split(jax.random.fold_in(key, 105), N_NODE)
    orders = jax.vmap(lambda one_key: jax.random.permutation(one_key, RESP_NODE))(order_keys).astype(jnp.int32)
    lens = jnp.take_along_axis(paired, orders, axis=1).astype(jnp.int32)
    edges = jnp.concatenate([jnp.zeros((N_NODE, 1), jnp.int32), jnp.cumsum(lens, axis=1).astype(jnp.int32)], axis=1)
    cuts = edges[:, 1:-1]
    local_id = jnp.sum((cuts[:, None, :] <= live_rank[:, :, None]).astype(jnp.int32), axis=2)
    global_id = local_id + jnp.arange(N_NODE, dtype=jnp.int32)[:, None] * RESP_NODE
    resp_rows = jnp.where(row_live, global_id, RESP).astype(jnp.int32).reshape(TOKENS)
    lengths = lens.reshape(RESP)
    return (resp_rows, plan, lengths)


def draw_resp_of_row(key, part):
    return layout(key)[0]


def draw_block_plan(key, part):
    return layout(key)[1]


def draw_resp_len(key, part):
    return layout(key)[2]


def draw_group_of_resp(key, part):
    key = jax.random.fold_in(key, 5)
    return (jax.random.permutation(key, RESP) // GSIZE).astype(jnp.int32)


def raised(result, key, source, target, parts, factor):
    owner, partner = [(jnp.arange(result.shape[dim]) // (result.shape[dim] // parts)).reshape([-1 if axis == dim else 1 for axis in range(result.ndim)]) for dim in (source, target)]
    chosen = jax.random.permutation(key, parts)[partner]
    strong = (owner == chosen) | (owner == (partner + parts // 2) % parts)
    return jnp.where(strong, factor * result, result)


def levels(key, dims, shards, low, largest):
    factor_of, own = 1.0, jax.random.fold_in(key, 6)
    for dim, shards_of in shards:
        draws = jnp.exp(jax.random.uniform(jax.random.fold_in(own, dim), (shards_of,), jnp.float32, low / len(shards), largest / len(shards)))
        factor_of = factor_of * jnp.repeat(draws, dims[dim] // shards_of).reshape([-1 if axis == dim else 1 for axis in range(len(dims))])
    return factor_of


def scatter_about(rng, dims, scale, limit, pieces=(), held_as=jnp.bfloat16):
    array = scale * jax.random.normal(rng, dims, jnp.float32)
    if pieces:
        array = array * levels(rng, dims, pieces, -0.22, 0.18)
    return jnp.clip(array, -limit, limit).astype(held_as)


def bell_draw_with(own_key, extent, scale, limit, cuts, heavy, kind=jnp.bfloat16):
    array = scale * jax.random.normal(own_key, extent, jnp.float32)
    if cuts:
        array = array * levels(own_key, extent, cuts, -0.22, 0.18)
    return jnp.clip(raised(array, jax.random.fold_in(own_key, 3), *heavy), -limit, limit).astype(kind)


def setup_inputs(seed: int = 0) -> dict:
    streams_of = jax.random.split(jax.random.key(seed), 11)
    x_rows = scatter_about(streams_of[0], (TOKENS, D), 1.0, 6.0, ((0, 256),))
    value_cot = scatter_about(streams_of[1], (TOKENS, KV), 8.0, 48.0, ((0, 256),))
    value_weight = scatter_about(streams_of[2], (D, KV), (KV // 8) ** -0.5, 0.5, ((0, 16),))
    resp_of_row = draw_resp_of_row(jax.random.fold_in(streams_of[10], 71), 0)
    block_plan = draw_block_plan(jax.random.fold_in(streams_of[10], 71), 0)
    resp_len = draw_resp_len(jax.random.fold_in(streams_of[10], 71), 0)
    group_of_resp = draw_group_of_resp(jax.random.fold_in(streams_of[10], 71), 0)
    rewards = scatter_about(streams_of[7], (RESP,), 1.0, 4.0, (), jnp.float32)
    send_error = bell_draw_with(streams_of[8], (N_NODE, D, KV), 2.0, 12.0, ((0, 16), (1, 16)), (0, 1, 16, 2.0))
    mean_error = scatter_about(streams_of[9], (N_CHIP, N_NODE, PIECE, KV), 1.0, 6.0, ((0, 16), (1, 16)), jnp.float32)
    return {"x_rows": x_rows, "value_cot": value_cot, "value_weight": value_weight, "resp_of_row": resp_of_row, "block_plan": block_plan, "resp_len": resp_len, "group_of_resp": group_of_resp, "rewards": rewards, "send_error": send_error, "mean_error": mean_error}


def squash(running):
    grouped = running.reshape(running.shape[0], running.shape[1] // 128, 128)
    magnitude = jnp.mean(jnp.abs(grouped), axis=2, keepdims=True) + 1e-6
    outgoing = (magnitude * jnp.tanh(grouped / magnitude)).reshape(running.shape).astype(jnp.bfloat16)
    return outgoing, running - outgoing.astype(jnp.float32)


def reference(x_rows, value_cot, value_weight, resp_of_row, block_plan, resp_len, group_of_resp, rewards, send_error, mean_error):
    group_ids = jnp.arange(GROUPS, dtype=jnp.int32)
    member = (group_of_resp[:, None] == group_ids[None, :]).astype(jnp.float32)
    group_mean = jnp.sum(member * rewards[:, None], axis=0) / GSIZE
    advantage = rewards - jnp.sum(member * group_mean[None, :], axis=1)
    lookup = jnp.concatenate([advantage / resp_len.astype(jnp.float32), jnp.zeros((1,), jnp.float32)])
    row_weight = lookup[resp_of_row]
    scaled = (row_weight[:, None] * value_cot.astype(jnp.float32)).astype(jnp.bfloat16)
    per_node = N_CHIP * NBLK
    input_blocks = x_rows.reshape(N_NODE, per_node, BLK * D)
    cot_blocks = scaled.reshape(N_NODE, per_node, BLK * KV)
    node_plans = block_plan.reshape(N_NODE, per_node, 3)
    targets = jnp.arange(N_CHIP * LIVE, dtype=jnp.int32)
    block_ids = jnp.arange(per_node, dtype=jnp.int32)

    def one_node(operands):
        input_part, cot_part, plan_part, error_part = operands
        target_slot = jnp.where(plan_part[:, 0] >= 0, plan_part[:, 0] * LIVE + plan_part[:, 2], -1).astype(jnp.int32)
        chosen = jnp.sum(jnp.where(target_slot[None, :] == targets[:, None], block_ids[None, :], 0), axis=1).astype(jnp.int32)
        packed_input = jnp.take(input_part, chosen, axis=0).reshape(N_CHIP * ROWS, D)
        packed_cot = jnp.take(cot_part, chosen, axis=0).reshape(N_CHIP * ROWS, KV)
        grad_rows = jnp.dot(packed_cot, value_weight.T, preferred_element_type=jnp.float32).astype(jnp.bfloat16)
        node_grad = jnp.dot(packed_input.T, packed_cot, preferred_element_type=jnp.float32)
        outgoing, leftover = squash(node_grad + error_part.astype(jnp.float32))
        return grad_rows, outgoing, leftover.astype(jnp.bfloat16)

    grad_rows, outgoing, new_send_error = lax.map(one_node, (input_blocks, cot_blocks, node_plans, send_error))
    node_mean = jnp.sum(outgoing, axis=0, dtype=jnp.float32) / N_NODE
    stored = mean_error.reshape(D, KV)
    update, remainder = squash(node_mean + stored)
    return grad_rows.reshape(DEVICES * ROWS, D), new_send_error, remainder.reshape(N_CHIP, N_NODE, PIECE, KV), update
```

```python
import functools

import jax
import jax.numpy as jnp
from jax import lax
from jax.experimental import pallas as pl
from jax.experimental.pallas import tpu as pltpu
from jax.sharding import PartitionSpec as P

MESH = pl.DeviceIdType.MESH
GSIZE = 8
SIDE = 4
CHIPS = 16
BLK = 12
NBLK = 16
SLOT = 192
WORK = 144
KV = 1024
COLS = 768
PIECE = 48
DEPTH = 8

GROUPS = (
    ((1, 0), (3, 0), (0, 1), (0, 3)),
    ((2, 0), (0, 2)),
    ((1, 1), (3, 3)),
    ((1, 3), (3, 1)),
    ((2, 2),),
    ((1, 2), (3, 2), (2, 1), (2, 3)),
)
ALL = tuple(o for group in GROUPS for o in group)
Z_ORDER = (4, 3, 5, 2, 6, 1, 7)


def squash(e):
    sent, left = [], []
    for j in range(KV // 128):
        g = e[:, 128 * j : 128 * (j + 1)]
        m = jnp.mean(jnp.abs(g), axis=1, keepdims=True) + 1e-06
        s = (m * jnp.tanh(g * (1.0 / m))).astype(jnp.bfloat16)
        sent.append(s)
        left.append(g - s.astype(jnp.float32))
    return sent, left


def row_weights(resp, rlen, grp, rew):
    resp_total = rew.shape[1]
    groups = resp_total // GSIZE
    member = lax.broadcasted_iota(jnp.int32, (groups, resp_total), 0) == grp
    mean = jnp.sum(jnp.where(member, rew, 0.0), axis=1, keepdims=True) / GSIZE
    advantage = rew - jnp.sum(jnp.where(member, mean, 0.0), axis=0, keepdims=True)
    lookup = advantage / rlen.astype(jnp.float32)
    ids = lax.broadcasted_iota(jnp.int32, (SLOT, resp_total), 1)
    return jnp.sum(jnp.where(resp == ids, lookup, 0.0), axis=1, keepdims=True)


def kernel(
    x_hbm, cot_hbm, w_hbm, resp_ref, plan_ref, rlen_ref, grp_ref, rew_ref, serr_hbm, merr_hbm,
    ig_out, nse_out, nme_out, upd_out,
    cot, w, serr, merr, cbuf, cf, xr, stage, gbuf, acc, sbuf, sib, zs, zr, pbuf, chv, chs,
    lsem, csend, crecv, xsend, xrecv, psend, precv, gsend, grecv,
    ssend, srecv, zsend, zrecv, usend, urecv, fsend, frecv,
):
    node, chip = lax.axis_index("node"), lax.axis_index("chip")
    y, x = chip // SIDE, lax.rem(chip, SIDE)
    z, core = node // 2, lax.rem(node, 2)
    other = 1 - core

    def plane(dx, dy):
        return lax.rem(y + dy, SIDE) * SIDE + lax.rem(x + dx, SIDE)

    def deep(dz):
        return lax.rem(z + dz, DEPTH)

    def remote(src, dst, send, recv, node_to, chip_to):
        return pltpu.make_async_remote_copy(
            src_ref=src, dst_ref=dst, send_sem=send, recv_sem=recv,
            device_id=(node_to, chip_to), device_id_type=MESH,
        )

    barrier = pltpu.get_barrier_semaphore()
    for dx, dy in ALL:
        pl.semaphore_signal(barrier, 1, device_id=(node, plane(dx, dy)), device_id_type=MESH)
    for dz in Z_ORDER:
        pl.semaphore_signal(barrier, 1, device_id=(deep(dz) * 2 + core, chip), device_id_type=MESH)
    pl.semaphore_signal(barrier, 1, device_id=(z * 2 + other, chip), device_id_type=MESH)

    loads = [
        pltpu.make_async_copy(cot_hbm, cot, lsem.at[0]),
        pltpu.make_async_copy(w_hbm, w, lsem.at[1]),
        pltpu.make_async_copy(serr_hbm, serr, lsem.at[2]),
        pltpu.make_async_copy(merr_hbm, merr, lsem.at[3]),
        pltpu.make_async_copy(
            x_hbm.at[:, pl.ds(pl.multiple_of(chip * COLS, 128), COLS)], xr.at[chip], lsem.at[4]
        ),
    ]
    for load in loads:
        load.start()

    weight = row_weights(resp_ref[...], rlen_ref[...], grp_ref[...], rew_ref[...])
    goes = plan_ref[...]
    target = jnp.where(goes[:, 0:1] >= 0, goes[:, 0:1] * (WORK // BLK) + goes[:, 2:3], -1)
    pbuf[chip] = jnp.broadcast_to(target, (NBLK, 128))
    loads[0].wait()
    cbuf[y, x] = (weight * cot[...].astype(jnp.float32)).astype(jnp.bfloat16)

    pl.semaphore_wait(barrier, len(ALL) + len(Z_ORDER) + 1)

    xp, xm = lax.rem(x + 1, SIDE), lax.rem(x + 3, SIDE)
    yp, ym = lax.rem(y + 1, SIDE), lax.rem(y + 3, SIDE)
    half, quarter = SLOT // 2, SLOT // 4

    def hop(i, block, to_y, to_x):
        return remote(block, block, csend.at[i], crecv.at[i], node, to_y * SIDE + to_x)

    lo, hi = pl.ds(0, half), pl.ds(half, half)
    q0, q1, q2, q3 = (pl.ds(quarter * i, quarter) for i in range(4))
    c = [
        hop(0, cbuf.at[y, x, lo], y, xp),
        hop(1, cbuf.at[y, x, lo], y, xm),
        hop(2, cbuf.at[y, x, hi], yp, x),
        hop(3, cbuf.at[y, x, hi], ym, x),
        hop(4, cbuf.at[y, xm, q0], y, xp),
        hop(5, cbuf.at[y, xp, q1], y, xm),
        hop(6, cbuf.at[ym, x, q2], yp, x),
        hop(7, cbuf.at[yp, x, q3], ym, x),
        hop(8, cbuf.at[y, :, lo], yp, x),
        hop(9, cbuf.at[y, :, lo], ym, x),
        hop(10, cbuf.at[:, x, hi], y, xp),
        hop(11, cbuf.at[:, x, hi], y, xm),
        hop(12, cbuf.at[ym, :, q0], yp, x),
        hop(13, cbuf.at[yp, :, q1], ym, x),
        hop(14, cbuf.at[:, xm, q2], y, xp),
        hop(15, cbuf.at[:, xp, q3], y, xm),
    ]

    def columns(dx, dy):
        to = plane(dx, dy)
        i = dy * SIDE + dx
        return remote(
            x_hbm.at[:, pl.ds(pl.multiple_of(to * COLS, 128), COLS)], xr.at[chip],
            xsend.at[i], xrecv.at[i], node, to,
        )

    def plans(dx, dy):
        i = dy * SIDE + dx
        return remote(pbuf.at[chip], pbuf.at[chip], psend.at[i], precv.at[i], node, plane(dx, dy))

    xs = {o: columns(*o) for o in ALL}
    ps = [plans(*o) for o in ALL]

    for i in (0, 1, 2, 3):
        c[i].start()
    for p in ps:
        p.start()
    for o in GROUPS[0]:
        xs[o].start()
    for i in (0, 1, 2, 3):
        c[i].wait_recv()
        c[i + 4].start()
    for i in (4, 5):
        c[i].wait_recv()
    c[8].start()
    c[9].start()
    for i in (6, 7):
        c[i].wait_recv()
    c[10].start()
    c[11].start()
    for o in GROUPS[1] + GROUPS[2]:
        xs[o].start()
    for i in (8, 9, 10, 11):
        c[i].wait_recv()
        c[i + 4].start()
    for o in GROUPS[3] + GROUPS[4] + GROUPS[5]:
        xs[o].start()

    for p in ps:
        p.wait_recv()
    where = pbuf[...].reshape(CHIPS * NBLK, 128)
    block = lax.broadcasted_iota(jnp.int32, (CHIPS * NBLK, 128), 0)
    lane = lax.broadcasted_iota(jnp.int32, (CHIPS * NBLK, 128), 1)
    chv[:, 0:128] = jnp.max(jnp.where(where == lane, block, 0), axis=0, keepdims=True)
    chv[:, 128:256] = jnp.max(jnp.where(where == lane + 128, block, 0), axis=0, keepdims=True)
    choose = pltpu.make_async_copy(chv, chs, lsem.at[5])
    choose.start()
    choose.wait()

    for i in (12, 13, 14, 15):
        c[i].wait_recv()
    loads[1].wait()

    def widen(s, carry):
        rows = cbuf[s // SIDE, lax.rem(s, SIDE)].astype(jnp.float32)
        for j in range(NBLK):
            cf[s * NBLK + j] = rows[j * BLK : (j + 1) * BLK]
        return carry

    lax.fori_loop(0, CHIPS, widen, 0)

    two = 2 * WORK // BLK

    def input_grad(s, carry):
        for j in range(two):
            b = chs[0, s * two + j]
            stage[pl.ds(j * BLK, BLK), :] = cf[b]
        rows = lax.dot_general(
            stage[...].astype(jnp.bfloat16), w[...], (((1,), (1,)), ((), ())),
            preferred_element_type=jnp.float32,
        )
        gbuf[pl.ds(2 * s, 2)] = rows.astype(jnp.bfloat16).reshape(2, WORK, COLS)
        return carry

    lax.fori_loop(0, CHIPS // 2, input_grad, 0)

    def owners(dx, dy):
        to = plane(dx, dy)
        i = dy * SIDE + dx
        return remote(
            gbuf.at[to], ig_out.at[:, pl.ds(pl.multiple_of(chip * COLS, 128), COLS)],
            gsend.at[i], grecv.at[i], node, to,
        )

    own_grad = pltpu.make_async_copy(
        gbuf.at[chip], ig_out.at[:, pl.ds(pl.multiple_of(chip * COLS, 128), COLS)], lsem.at[6]
    )
    own_grad.start()
    for o in ALL:
        xs[o].wait_send()
    gs = [owners(*o) for o in ALL]
    for g in gs:
        g.start()

    loads[4].wait()
    for o in ALL:
        xs[o].wait_recv()
    acc[...] = jnp.zeros_like(acc)

    def contract(s, carry):
        acc[...] += lax.dot_general(
            xr[pl.ds(s * SIDE, SIDE)].reshape(SIDE * SLOT, COLS), cbuf[s].reshape(SIDE * SLOT, KV),
            (((0,), (0,)), ((), ())), preferred_element_type=jnp.float32,
        )
        return carry

    lax.fori_loop(0, SIDE, contract, 0)

    loads[2].wait()

    def compress(which):
        def one(k, carry):
            p = pl.multiple_of((k * 2 + which) * PIECE, PIECE)
            e = acc[pl.ds(p, PIECE), :] + serr[pl.ds(p, PIECE), :].astype(jnp.float32)
            sent, left = squash(e)
            for j in range(KV // 128):
                sbuf[which, k, :, 128 * j : 128 * (j + 1)] = sent[j]
                nse_out[pl.ds(p, PIECE), 128 * j : 128 * (j + 1)] = left[j].astype(jnp.bfloat16)
            return carry

        lax.fori_loop(0, DEPTH, one, 0)

    compress(other)
    pair = remote(sbuf.at[other], sib, ssend, srecv, z * 2 + other, chip)
    pair.start()
    compress(core)
    pair.wait_recv()

    zc = {}
    for dz in Z_ORDER:
        to = deep(dz)
        zs[to] = (sbuf[core, to].astype(jnp.float32) + sib[to].astype(jnp.float32)).astype(jnp.bfloat16)
        zc[dz] = remote(zs.at[to], zr.at[dz], zsend.at[dz], zrecv.at[dz], to * 2 + core, chip)
        zc[dz].start()
    total = sbuf[core, z].astype(jnp.float32) + sib[z].astype(jnp.float32)
    for dz in reversed(Z_ORDER):
        zc[dz].wait_recv()
        total = total + zr[dz].astype(jnp.float32)
    loads[3].wait()
    sent, left = squash(total * (1.0 / 16) + merr[...])
    for j in range(KV // 128):
        upd_out[node, :, 128 * j : 128 * (j + 1)] = sent[j]
        nme_out[:, 128 * j : 128 * (j + 1)] = left[j]

    us = {}
    for dz in Z_ORDER:
        us[dz] = remote(
            upd_out.at[node], upd_out.at[node], usend.at[dz], urecv.at[dz], deep(dz) * 2 + core, chip
        )
        us[dz].start()
    fs = []

    def share(i, n):
        f = remote(upd_out.at[n], upd_out.at[n], fsend.at[i], frecv.at[i], z * 2 + other, chip)
        f.start()
        fs.append(f)

    share(0, node)
    for dz in reversed(Z_ORDER):
        us[dz].wait_recv()
        share(dz, deep(DEPTH - dz) * 2 + core)
    for f in fs:
        f.wait_recv()
    own_grad.wait()
    for g in gs:
        g.wait_recv()
    for s in c + ps + gs + fs + [pair] + list(zc.values()) + list(us.values()):
        s.wait_send()


def per_device(
    x_rows, value_cot, value_weight, resp_of_row, block_plan, resp_len, group_of_resp, rewards, send_error, mean_error
):
    vmem = pl.BlockSpec(memory_space=pltpu.VMEM)
    hbm = pl.BlockSpec(memory_space=pl.ANY)
    bf16, f32, i32 = jnp.bfloat16, jnp.float32, jnp.int32
    dma = pltpu.SemaphoreType.DMA
    ig, nse, nme, upd = pl.pallas_call(
        kernel,
        out_shape=(
            jax.ShapeDtypeStruct((WORK, CHIPS * COLS), bf16),
            jax.ShapeDtypeStruct((COLS, KV), bf16),
            jax.ShapeDtypeStruct((PIECE, KV), f32),
            jax.ShapeDtypeStruct((CHIPS, PIECE, KV), bf16),
        ),
        in_specs=[hbm, hbm, hbm, vmem, vmem, vmem, vmem, vmem, hbm, hbm],
        out_specs=(hbm, vmem, vmem, vmem),
        scratch_shapes=[
            pltpu.VMEM((SLOT, KV), bf16),
            pltpu.VMEM((COLS, KV), bf16),
            pltpu.VMEM((COLS, KV), bf16),
            pltpu.VMEM((PIECE, KV), f32),
            pltpu.VMEM((SIDE, SIDE, SLOT, KV), bf16),
            pltpu.VMEM((CHIPS * NBLK, BLK, KV), f32),
            pltpu.VMEM((CHIPS, SLOT, COLS), bf16),
            pltpu.VMEM((2 * WORK, KV), f32),
            pltpu.VMEM((CHIPS, WORK, COLS), bf16),
            pltpu.VMEM((COLS, KV), f32),
            pltpu.VMEM((2, DEPTH, PIECE, KV), bf16),
            pltpu.VMEM((DEPTH, PIECE, KV), bf16),
            pltpu.VMEM((DEPTH, PIECE, KV), bf16),
            pltpu.VMEM((DEPTH, PIECE, KV), bf16),
            pltpu.VMEM((CHIPS, NBLK, 128), i32),
            pltpu.VMEM((1, 256), i32),
            pltpu.SMEM((1, 256), i32),
            dma((8,)), dma((16,)), dma((16,)), dma((16,)), dma((16,)), dma((16,)), dma((16,)),
            dma((16,)), dma((16,)), dma, dma, dma((8,)), dma((8,)), dma((8,)), dma((8,)),
            dma((8,)), dma((8,)),
        ],
        compiler_params=pltpu.CompilerParams(
            collective_id=0, has_side_effects=True, vmem_limit_bytes=58 * 2**20
        ),
        cost_estimate=pl.CostEstimate(flops=8_000_000_000, bytes_accessed=20_000_000, transcendentals=800_000),
    )(
        x_rows, value_cot, value_weight, resp_of_row.reshape(SLOT, 1), block_plan,
        resp_len.reshape(1, -1), group_of_resp.reshape(1, -1), rewards.reshape(1, -1),
        send_error.reshape(COLS, KV), mean_error.reshape(PIECE, KV),
    )
    return ig, nse[None], nme[None, None], upd.reshape(COLS, KV)


def solution(mesh):
    return jax.shard_map(
        per_device,
        mesh=mesh,
        in_specs=(
            P(("node", "chip"), None),
            P(("node", "chip"), None),
            P("chip", None),
            P(("node", "chip")),
            P(("node", "chip"), None),
            P(),
            P(),
            P(),
            P("node", "chip", None),
            P("chip", "node", None, None),
        ),
        out_specs=(
            P(("node", "chip"), None),
            P("node", "chip", None),
            P("chip", "node", None, None),
            P("chip", None),
        ),
        check_vma=False,
    )
```

```python
import functools

import jax
import jax.numpy as jnp
from jax import lax
from jax.experimental import pallas as pl
from jax.experimental.pallas import tpu as pltpu
from jax.sharding import PartitionSpec as P

MESH = pl.DeviceIdType.MESH
GSIZE = 8
SIDE = 4
CHIPS = 16
BLK = 12
NBLK = 16
SLOT = 192
WORK = 144
KV = 1024
COLS = 768
PIECE = 48
DEPTH = 8
HALF = KV // 2

GROUPS = (
    ((1, 0), (3, 0), (0, 1), (0, 3)),
    ((2, 0), (0, 2)),
    ((1, 1), (3, 3)),
    ((1, 3), (3, 1)),
    ((2, 1), (2, 3)),
    ((2, 2),),
    ((1, 2), (3, 2)),
)
ALL = tuple(o for group in GROUPS for o in group)
Z_ORDER = (4, 3, 5, 2, 6, 1, 7)


def squash(e):
    sent, left = [], []
    for j in range(e.shape[1] // 128):
        g = e[:, 128 * j : 128 * (j + 1)]
        m = jnp.mean(jnp.abs(g), axis=1, keepdims=True) + 1e-06
        s = (m * jnp.tanh(g * (1.0 / m))).astype(jnp.bfloat16)
        sent.append(s)
        left.append(g - s.astype(jnp.float32))
    return sent, left


def upright(row):
    n = row.shape[1]
    here = lax.broadcasted_iota(jnp.int32, (n, n), 0) == lax.broadcasted_iota(jnp.int32, (n, n), 1)
    return jnp.sum(jnp.where(here, row, 0), axis=1, keepdims=True)


def row_weights(resp, rlen, grp, rew):
    resp_total = rew.shape[1]
    groups = resp_total // GSIZE
    member = lax.broadcasted_iota(jnp.int32, (groups, resp_total), 0) == grp
    mean = jnp.sum(jnp.where(member, rew, 0.0), axis=1, keepdims=True) / GSIZE
    advantage = rew - jnp.sum(jnp.where(member, mean, 0.0), axis=0, keepdims=True)
    lookup = advantage / rlen.astype(jnp.float32)
    ids = lax.broadcasted_iota(jnp.int32, (SLOT, resp_total), 1)
    return jnp.sum(jnp.where(resp == ids, lookup, 0.0), axis=1, keepdims=True)


def kernel(
    x_hbm, cot_hbm, w_hbm, resp_ref, plan_ref, rlen_ref, grp_ref, rew_ref, serr_hbm, merr_hbm,
    ig_out, nse_out, nme_out, upd_out,
    cot, w, serr, merr, cbuf, cf, xr, stage, gbuf, acc, sbuf, sib, zs, zr, pbuf, chv, chs,
    lsem, csend, crecv, xsend, xrecv, psend, precv, gsend, grecv,
    ssend, srecv, zsend, zrecv, usend, urecv, fsend, frecv,
):
    node, chip = lax.axis_index("node"), lax.axis_index("chip")
    y, x = chip // SIDE, lax.rem(chip, SIDE)
    z, core = node // 2, lax.rem(node, 2)
    other = 1 - core

    def plane(dx, dy):
        return lax.rem(y + dy, SIDE) * SIDE + lax.rem(x + dx, SIDE)

    def deep(dz):
        return lax.rem(z + dz, DEPTH)

    def remote(src, dst, send, recv, node_to, chip_to):
        return pltpu.make_async_remote_copy(
            src_ref=src, dst_ref=dst, send_sem=send, recv_sem=recv,
            device_id=(node_to, chip_to), device_id_type=MESH,
        )

    barrier = pltpu.get_barrier_semaphore()
    for dx, dy in ALL:
        pl.semaphore_signal(barrier, 1, device_id=(node, plane(dx, dy)), device_id_type=MESH)
    for dz in Z_ORDER:
        pl.semaphore_signal(barrier, 1, device_id=(deep(dz) * 2 + core, chip), device_id_type=MESH)
    pl.semaphore_signal(barrier, 1, device_id=(z * 2 + other, chip), device_id_type=MESH)

    loads = [
        pltpu.make_async_copy(cot_hbm, cot, lsem.at[0]),
        pltpu.make_async_copy(w_hbm, w, lsem.at[1]),
        pltpu.make_async_copy(serr_hbm, serr, lsem.at[2]),
        pltpu.make_async_copy(merr_hbm, merr, lsem.at[3]),
        pltpu.make_async_copy(
            x_hbm.at[:, pl.ds(pl.multiple_of(chip * COLS, 128), COLS)], xr.at[chip], lsem.at[4]
        ),
    ]
    for load in loads:
        load.start()

    weight = row_weights(upright(resp_ref[...]), rlen_ref[...], grp_ref[...], rew_ref[...])
    goes = plan_ref[...]
    target = jnp.where(goes[0:1] >= 0, goes[0:1] * (WORK // BLK) + goes[2:3], -1)
    pbuf[chip] = jnp.broadcast_to(upright(target), (NBLK, 128))
    loads[0].wait()
    cbuf[y, x] = (weight * cot[...].astype(jnp.float32)).astype(jnp.bfloat16)

    pl.semaphore_wait(barrier, len(ALL) + len(Z_ORDER) + 1)

    xp, xm = lax.rem(x + 1, SIDE), lax.rem(x + 3, SIDE)
    yp, ym = lax.rem(y + 1, SIDE), lax.rem(y + 3, SIDE)
    half, quarter = SLOT // 2, SLOT // 4

    def hop(i, block, to_y, to_x):
        return remote(block, block, csend.at[i], crecv.at[i], node, to_y * SIDE + to_x)

    lo, hi = pl.ds(0, half), pl.ds(half, half)
    q0, q1, q2, q3 = (pl.ds(quarter * i, quarter) for i in range(4))
    c = [
        hop(0, cbuf.at[y, x, lo], y, xp),
        hop(1, cbuf.at[y, x, lo], y, xm),
        hop(2, cbuf.at[y, x, hi], yp, x),
        hop(3, cbuf.at[y, x, hi], ym, x),
        hop(4, cbuf.at[y, xm, q0], y, xp),
        hop(5, cbuf.at[y, xp, q1], y, xm),
        hop(6, cbuf.at[ym, x, q2], yp, x),
        hop(7, cbuf.at[yp, x, q3], ym, x),
        hop(8, cbuf.at[y, :, lo], yp, x),
        hop(9, cbuf.at[y, :, lo], ym, x),
        hop(10, cbuf.at[:, x, hi], y, xp),
        hop(11, cbuf.at[:, x, hi], y, xm),
        hop(12, cbuf.at[ym, :, q0], yp, x),
        hop(13, cbuf.at[yp, :, q1], ym, x),
        hop(14, cbuf.at[:, xm, q2], y, xp),
        hop(15, cbuf.at[:, xp, q3], y, xm),
    ]

    def columns(dx, dy):
        to = plane(dx, dy)
        i = dy * SIDE + dx
        return remote(
            x_hbm.at[:, pl.ds(pl.multiple_of(to * COLS, 128), COLS)], xr.at[chip],
            xsend.at[i], xrecv.at[i], node, to,
        )

    def plans(dx, dy):
        i = dy * SIDE + dx
        return remote(pbuf.at[chip], pbuf.at[chip], psend.at[i], precv.at[i], node, plane(dx, dy))

    xs = {o: columns(*o) for o in ALL}
    ps = [plans(*o) for o in ALL]

    for i in (0, 1, 2, 3):
        c[i].start()
    for p in ps:
        p.start()
    for o in GROUPS[0]:
        xs[o].start()
    for i in (0, 1, 2, 3):
        c[i].wait_recv()
        c[i + 4].start()
    for i in (4, 5):
        c[i].wait_recv()
    c[8].start()
    c[9].start()
    for i in (6, 7):
        c[i].wait_recv()
    c[10].start()
    c[11].start()
    for o in GROUPS[1] + GROUPS[2]:
        xs[o].start()
    for i in (8, 9, 10, 11):
        c[i].wait_recv()
        c[i + 4].start()
    for o in GROUPS[3] + GROUPS[4] + GROUPS[5] + GROUPS[6]:
        xs[o].start()

    for p in ps:
        p.wait_recv()
    where = pbuf[...].reshape(CHIPS * NBLK, 128)
    block = lax.broadcasted_iota(jnp.int32, (CHIPS * NBLK, 128), 0)
    lane = lax.broadcasted_iota(jnp.int32, (CHIPS * NBLK, 128), 1)
    chv[:, 0:128] = jnp.max(jnp.where(where == lane, block, 0), axis=0, keepdims=True)
    chv[:, 128:256] = jnp.max(jnp.where(where == lane + 128, block, 0), axis=0, keepdims=True)
    choose = pltpu.make_async_copy(chv, chs, lsem.at[5])
    choose.start()
    choose.wait()

    for i in (12, 13, 14, 15):
        c[i].wait_recv()
    loads[1].wait()

    def widen(s, carry):
        rows = cbuf[s // SIDE, lax.rem(s, SIDE)].astype(jnp.float32)
        for j in range(NBLK):
            cf[s * NBLK + j] = rows[j * BLK : (j + 1) * BLK]
        return carry

    lax.fori_loop(0, CHIPS, widen, 0)

    two = 2 * WORK // BLK

    def input_grad(s, carry):
        for j in range(two):
            b = chs[0, s * two + j]
            stage[pl.ds(j * BLK, BLK), :] = cf[b]
        rows = lax.dot_general(
            stage[...].astype(jnp.bfloat16), w[...], (((1,), (1,)), ((), ())),
            preferred_element_type=jnp.float32,
        )
        gbuf[pl.ds(2 * s, 2)] = rows.astype(jnp.bfloat16).reshape(2, WORK, COLS)
        return carry

    lax.fori_loop(0, CHIPS // 2, input_grad, 0)

    def owners(dx, dy):
        to = plane(dx, dy)
        i = dy * SIDE + dx
        return remote(
            gbuf.at[to], ig_out.at[:, pl.ds(pl.multiple_of(chip * COLS, 128), COLS)],
            gsend.at[i], grecv.at[i], node, to,
        )

    own_grad = pltpu.make_async_copy(
        gbuf.at[chip], ig_out.at[:, pl.ds(pl.multiple_of(chip * COLS, 128), COLS)], lsem.at[6]
    )
    own_grad.start()
    for o in ALL:
        xs[o].wait_send()
    gs = [owners(*o) for o in ALL]
    for g in gs:
        g.start()

    loads[4].wait()
    loads[2].wait()
    loads[3].wait()

    def contract(dy, cols):
        s = lax.rem(y + SIDE - dy, SIDE)
        part = lax.dot_general(
            xr[pl.ds(s * SIDE, SIDE)].reshape(SIDE * SLOT, COLS),
            cbuf[s, :, :, cols].reshape(SIDE * SLOT, cols.stop - cols.start),
            (((0,), (0,)), ((), ())), preferred_element_type=jnp.float32,
        )
        if dy == 0:
            acc[:, cols] = part
        else:
            acc[:, cols] += part

    for dy in (0, 1, 3, 2):
        for dx in range(SIDE):
            if (dx, dy) != (0, 0):
                xs[dx, dy].wait_recv()
        if dy != 2:
            contract(dy, slice(0, KV))

    def compress(which, h):
        def one(k, carry):
            p = pl.multiple_of((k * 2 + which) * PIECE, PIECE)
            cols = slice(h * HALF, (h + 1) * HALF)
            e = acc[pl.ds(p, PIECE), cols] + serr[pl.ds(p, PIECE), cols].astype(jnp.float32)
            sent, left = squash(e)
            for j in range(HALF // 128):
                sbuf[h, which, k, :, 128 * j : 128 * (j + 1)] = sent[j]
                at = h * HALF + 128 * j
                nse_out[pl.ds(p, PIECE), at : at + 128] = left[j].astype(jnp.bfloat16)
            return carry

        lax.fori_loop(0, DEPTH, one, 0)

    pair, zc = [], [{}, {}]
    for h in (0, 1):
        contract(2, slice(h * HALF, (h + 1) * HALF))
        compress(other, h)
        pair.append(remote(sbuf.at[h, other], sib.at[h], ssend.at[h], srecv.at[h], z * 2 + other, chip))
        pair[h].start()
        compress(core, h)
        pair[h].wait_recv()
        for dz in Z_ORDER:
            to = deep(dz)
            zs[h, to] = (
                sbuf[h, core, to].astype(jnp.float32) + sib[h, to].astype(jnp.float32)
            ).astype(jnp.bfloat16)
            zc[h][dz] = remote(
                zs.at[h, to], zr.at[h, dz], zsend.at[h, dz], zrecv.at[h, dz], to * 2 + core, chip
            )
            zc[h][dz].start()

    sent_on = []

    def ring(h, step, up):
        n = deep(DEPTH - step if up else step) * 2 + core
        cols = pl.ds(h * HALF, HALF)
        if step == 3:
            cols = pl.ds(h * HALF + (0 if up else HALF // 2), HALF // 2)
        i = (h * 4 + step) * 2 + (1 if up else 0)
        return remote(
            upd_out.at[n, :, cols], upd_out.at[n, :, cols], usend.at[i], urecv.at[i],
            deep(1 if up else DEPTH - 1) * 2 + core, chip,
        )

    def share(h, dz):
        n = deep(dz) * 2 + core
        block = upd_out.at[n, :, pl.ds(h * HALF, HALF)]
        i = h * DEPTH + dz
        f = remote(block, block, fsend.at[i], frecv.at[i], z * 2 + other, chip)
        f.start()
        return f

    us, fs = {}, []

    def average(h):
        cols = slice(h * HALF, (h + 1) * HALF)
        total = sbuf[h, core, z].astype(jnp.float32) + sib[h, z].astype(jnp.float32)
        for dz in reversed(Z_ORDER):
            zc[h][dz].wait_recv()
            total = total + zr[h, dz].astype(jnp.float32)
        sent, left = squash(total * (1.0 / 16) + merr[:, cols])
        for j in range(HALF // 128):
            at = h * HALF + 128 * j
            upd_out[node, :, at : at + 128] = sent[j]
            nme_out[:, at : at + 128] = left[j]
        forward(h, 0)
        fs.append(share(h, 0))

    def forward(h, step):
        for up in (True, False):
            if step:
                us[h, step - 1, up].wait_recv()
            if step < 4:
                us[h, step, up] = ring(h, step, up)
                us[h, step, up].start()
        if step in (1, 2, 3):
            fs.append(share(h, DEPTH - step))
            fs.append(share(h, step))
        elif step == 4:
            fs.append(share(h, 4))

    average(0)
    forward(0, 1)
    average(1)
    for step in (2, 3, 4):
        forward(0, step)
        forward(1, step - 1)
    forward(1, 4)
    for f in fs:
        f.wait_recv()
    own_grad.wait()
    for g in gs:
        g.wait_recv()
    for s in c + ps + gs + fs + pair + list(zc[0].values()) + list(zc[1].values()) + list(us.values()):
        s.wait_send()


def leave(ig, nse, nme, upd, ig_out, nse_out, nme_out, upd_out, ig_v, nse_v, nme_v, upd_v, get, put):
    parts = []
    for src, mid, dst in ((ig, ig_v, ig_out), (nse, nse_v, nse_out), (upd, upd_v, upd_out), (nme, nme_v, nme_out)):
        step = min(src.shape[0], 2 * PIECE)
        for r in range(0, src.shape[0], step):
            n = min(step, src.shape[0] - r)
            parts.append([ref.at[pl.ds(r, n)] for ref in (src, mid, dst)])
    reads = [pltpu.make_async_copy(a, b, get.at[i]) for i, (a, b, _) in enumerate(parts)]
    writes = [pltpu.make_async_copy(b, c, put.at[i]) for i, (_, b, c) in enumerate(parts)]
    for read in reads:
        read.start()
    for read, write in zip(reads, writes):
        read.wait()
        write.start()
    for write in writes:
        write.wait()


def per_device(
    x_rows, value_cot, value_weight, resp_of_row, block_plan, resp_len, group_of_resp, rewards, send_error, mean_error
):
    vmem = pl.BlockSpec(memory_space=pltpu.VMEM)
    hbm = pl.BlockSpec(memory_space=pl.ANY)
    bf16, f32, i32 = jnp.bfloat16, jnp.float32, jnp.int32
    dma = pltpu.SemaphoreType.DMA
    ig, nse, nme, upd = pl.pallas_call(
        kernel,
        out_shape=(
            jax.ShapeDtypeStruct((WORK, CHIPS * COLS), bf16),
            jax.ShapeDtypeStruct((COLS, KV), bf16),
            jax.ShapeDtypeStruct((PIECE, KV), f32),
            jax.ShapeDtypeStruct((CHIPS, PIECE, KV), bf16),
        ),
        in_specs=[hbm, hbm, hbm, vmem, vmem, vmem, vmem, vmem, hbm, hbm],
        out_specs=(hbm, vmem, vmem, vmem),
        scratch_shapes=[
            pltpu.VMEM((SLOT, KV), bf16),
            pltpu.VMEM((COLS, KV), bf16),
            pltpu.VMEM((COLS, KV), bf16),
            pltpu.VMEM((PIECE, KV), f32),
            pltpu.VMEM((SIDE, SIDE, SLOT, KV), bf16),
            pltpu.VMEM((CHIPS * NBLK, BLK, KV), f32),
            pltpu.VMEM((CHIPS, SLOT, COLS), bf16),
            pltpu.VMEM((2 * WORK, KV), f32),
            pltpu.VMEM((CHIPS, WORK, COLS), bf16),
            pltpu.VMEM((COLS, KV), f32),
            pltpu.VMEM((2, 2, DEPTH, PIECE, HALF), bf16),
            pltpu.VMEM((2, DEPTH, PIECE, HALF), bf16),
            pltpu.VMEM((2, DEPTH, PIECE, HALF), bf16),
            pltpu.VMEM((2, DEPTH, PIECE, HALF), bf16),
            pltpu.VMEM((CHIPS, NBLK, 128), i32),
            pltpu.VMEM((1, 256), i32),
            pltpu.SMEM((1, 256), i32),
            dma((8,)), dma((16,)), dma((16,)), dma((16,)), dma((16,)), dma((16,)), dma((16,)),
            dma((16,)), dma((16,)), dma((2,)), dma((2,)), dma((2, 8)), dma((2, 8)), dma((16,)), dma((16,)),
            dma((16,)), dma((16,)),
        ],
        compiler_params=pltpu.CompilerParams(
            collective_id=0, has_side_effects=True, vmem_limit_bytes=58 * 2**20
        ),
        cost_estimate=pl.CostEstimate(flops=8_000_000_000, bytes_accessed=20_000_000, transcendentals=800_000),
    )(
        x_rows, value_cot, value_weight, resp_of_row.reshape(1, SLOT), block_plan.T,
        resp_len.reshape(1, -1), group_of_resp.reshape(1, -1), rewards.reshape(1, -1),
        send_error.reshape(COLS, KV), mean_error.reshape(PIECE, KV),
    )
    upd = upd.reshape(COLS, KV)
    ig, nse, nme, upd = pl.pallas_call(
        leave,
        out_shape=tuple(jax.ShapeDtypeStruct(a.shape, a.dtype) for a in (ig, nse, nme, upd)),
        in_specs=[hbm] * 4,
        out_specs=[hbm] * 4,
        scratch_shapes=[pltpu.VMEM(a.shape, a.dtype) for a in (ig, nse, nme, upd)] + [dma((24,)), dma((24,))],
        compiler_params=pltpu.CompilerParams(vmem_limit_bytes=58 * 2**20),
    )(ig, nse, nme, upd)
    return ig, nse[None], nme[None, None], upd


def solution(mesh):
    return jax.shard_map(
        per_device,
        mesh=mesh,
        in_specs=(
            P(("node", "chip"), None),
            P(("node", "chip"), None),
            P("chip", None),
            P(("node", "chip")),
            P(("node", "chip"), None),
            P(),
            P(),
            P(),
            P("node", "chip", None),
            P("chip", "node", None, None),
        ),
        out_specs=(
            P(("node", "chip"), None),
            P("node", "chip", None),
            P("chip", "node", None, None),
            P("chip", None),
        ),
        check_vma=False,
    )
```

```python
import functools

import jax
import jax.numpy as jnp
from jax import lax
from jax.experimental import pallas as pl
from jax.experimental.pallas import tpu as pltpu
from jax.sharding import PartitionSpec as P

MESH = pl.DeviceIdType.MESH
GSIZE = 8
SIDE = 4
CHIPS = 16
BLK = 12
NBLK = 16
SLOT = 192
WORK = 144
KV = 1024
COLS = 768
PIECE = 48
DEPTH = 8
HALF = KV // 2

GROUPS = (
    ((1, 0), (3, 0), (0, 1), (0, 3)),
    ((2, 0), (0, 2)),
    ((1, 1), (3, 3)),
    ((1, 3), (3, 1)),
    ((2, 1), (2, 3)),
    ((2, 2),),
    ((1, 2), (3, 2)),
)
ALL = tuple(o for group in GROUPS for o in group)
Z_ORDER = (4, 3, 5, 2, 6, 1, 7)


def squash(e):
    sent, left = [], []
    for j in range(e.shape[1] // 128):
        g = e[:, 128 * j : 128 * (j + 1)]
        m = jnp.mean(jnp.abs(g), axis=1, keepdims=True) + 1e-06
        s = (m * jnp.tanh(g * (1.0 / m))).astype(jnp.bfloat16)
        sent.append(s)
        left.append(g - s.astype(jnp.float32))
    return sent, left


def upright(row):
    n = row.shape[1]
    here = lax.broadcasted_iota(jnp.int32, (n, n), 0) == lax.broadcasted_iota(jnp.int32, (n, n), 1)
    return jnp.sum(jnp.where(here, row, 0), axis=1, keepdims=True)


def row_weights(resp, rlen, grp, rew):
    resp_total = rew.shape[1]
    groups = resp_total // GSIZE
    member = lax.broadcasted_iota(jnp.int32, (groups, resp_total), 0) == grp
    mean = jnp.sum(jnp.where(member, rew, 0.0), axis=1, keepdims=True) / GSIZE
    advantage = rew - jnp.sum(jnp.where(member, mean, 0.0), axis=0, keepdims=True)
    lookup = advantage / rlen.astype(jnp.float32)
    ids = lax.broadcasted_iota(jnp.int32, (SLOT, resp_total), 1)
    return jnp.sum(jnp.where(resp == ids, lookup, 0.0), axis=1, keepdims=True)


def kernel(
    x_hbm, cot_hbm, w_hbm, resp_ref, plan_ref, rlen_ref, grp_ref, rew_ref, serr_hbm, merr_hbm,
    ig_out, nse_out, nme_out, upd_out,
    cot, w, serr, merr, cbuf, cf, xr, stage, gbuf, acc, sbuf, sib, zs, zr, pbuf, chv, chs,
    lsem, csend, crecv, xsend, xrecv, psend, precv, gsend, grecv,
    ssend, srecv, zsend, zrecv, usend, urecv, fsend, frecv,
):
    node, chip = lax.axis_index("node"), lax.axis_index("chip")
    y, x = chip // SIDE, lax.rem(chip, SIDE)
    z, core = node // 2, lax.rem(node, 2)
    other = 1 - core

    def plane(dx, dy):
        return lax.rem(y + dy, SIDE) * SIDE + lax.rem(x + dx, SIDE)

    def deep(dz):
        return lax.rem(z + dz, DEPTH)

    def remote(src, dst, send, recv, node_to, chip_to):
        return pltpu.make_async_remote_copy(
            src_ref=src, dst_ref=dst, send_sem=send, recv_sem=recv,
            device_id=(node_to, chip_to), device_id_type=MESH,
        )

    barrier = pltpu.get_barrier_semaphore()
    for dx, dy in ALL:
        pl.semaphore_signal(barrier, 1, device_id=(node, plane(dx, dy)), device_id_type=MESH)
    for dz in Z_ORDER:
        pl.semaphore_signal(barrier, 1, device_id=(deep(dz) * 2 + core, chip), device_id_type=MESH)
    pl.semaphore_signal(barrier, 1, device_id=(z * 2 + other, chip), device_id_type=MESH)

    loads = [
        pltpu.make_async_copy(cot_hbm, cot, lsem.at[0]),
        pltpu.make_async_copy(w_hbm, w, lsem.at[1]),
        pltpu.make_async_copy(serr_hbm, serr, lsem.at[2]),
        pltpu.make_async_copy(merr_hbm, merr, lsem.at[3]),
        pltpu.make_async_copy(
            x_hbm.at[:, pl.ds(pl.multiple_of(chip * COLS, 128), COLS)], xr.at[chip], lsem.at[4]
        ),
    ]
    for load in loads:
        load.start()

    weight = row_weights(upright(resp_ref[...]), rlen_ref[...], grp_ref[...], rew_ref[...])
    goes = plan_ref[...]
    target = jnp.where(goes[0:1] >= 0, goes[0:1] * (WORK // BLK) + goes[2:3], -1)
    pbuf[chip] = jnp.broadcast_to(upright(target), (NBLK, 128))
    loads[0].wait()
    cbuf[y, x] = (weight * cot[...].astype(jnp.float32)).astype(jnp.bfloat16)

    pl.semaphore_wait(barrier, len(ALL) + len(Z_ORDER) + 1)

    xp, xm = lax.rem(x + 1, SIDE), lax.rem(x + 3, SIDE)
    yp, ym = lax.rem(y + 1, SIDE), lax.rem(y + 3, SIDE)
    half, quarter = SLOT // 2, SLOT // 4

    def hop(i, block, to_y, to_x):
        return remote(block, block, csend.at[i], crecv.at[i], node, to_y * SIDE + to_x)

    lo, hi = pl.ds(0, half), pl.ds(half, half)
    q0, q1, q2, q3 = (pl.ds(quarter * i, quarter) for i in range(4))
    c = [
        hop(0, cbuf.at[y, x, lo], y, xp),
        hop(1, cbuf.at[y, x, lo], y, xm),
        hop(2, cbuf.at[y, x, hi], yp, x),
        hop(3, cbuf.at[y, x, hi], ym, x),
        hop(4, cbuf.at[y, xm, q0], y, xp),
        hop(5, cbuf.at[y, xp, q1], y, xm),
        hop(6, cbuf.at[ym, x, q2], yp, x),
        hop(7, cbuf.at[yp, x, q3], ym, x),
        hop(8, cbuf.at[y, :, lo], yp, x),
        hop(9, cbuf.at[y, :, lo], ym, x),
        hop(10, cbuf.at[:, x, hi], y, xp),
        hop(11, cbuf.at[:, x, hi], y, xm),
        hop(12, cbuf.at[ym, :, q0], yp, x),
        hop(13, cbuf.at[yp, :, q1], ym, x),
        hop(14, cbuf.at[:, xm, q2], y, xp),
        hop(15, cbuf.at[:, xp, q3], y, xm),
    ]

    def columns(dx, dy):
        to = plane(dx, dy)
        i = dy * SIDE + dx
        return remote(
            x_hbm.at[:, pl.ds(pl.multiple_of(to * COLS, 128), COLS)], xr.at[chip],
            xsend.at[i], xrecv.at[i], node, to,
        )

    def plans(dx, dy):
        i = dy * SIDE + dx
        return remote(pbuf.at[chip], pbuf.at[chip], psend.at[i], precv.at[i], node, plane(dx, dy))

    xs = {o: columns(*o) for o in ALL}
    ps = [plans(*o) for o in ALL]

    for i in (0, 1, 2, 3):
        c[i].start()
    for p in ps:
        p.start()
    for o in GROUPS[0] + GROUPS[1] + GROUPS[2]:
        xs[o].start()
    for i in (0, 1, 2, 3):
        c[i].wait_recv()
        c[i + 4].start()
    for i in (4, 5):
        c[i].wait_recv()
    c[8].start()
    c[9].start()
    for i in (6, 7):
        c[i].wait_recv()
    c[10].start()
    c[11].start()
    for o in GROUPS[3] + GROUPS[4]:
        xs[o].start()
    for i in (8, 9, 10, 11):
        c[i].wait_recv()
        c[i + 4].start()
    for o in GROUPS[5] + GROUPS[6]:
        xs[o].start()

    for p in ps:
        p.wait_recv()
    where = pbuf[...].reshape(CHIPS * NBLK, 128)
    block = lax.broadcasted_iota(jnp.int32, (CHIPS * NBLK, 128), 0)
    lane = lax.broadcasted_iota(jnp.int32, (CHIPS * NBLK, 128), 1)
    chv[:, 0:128] = jnp.max(jnp.where(where == lane, block, 0), axis=0, keepdims=True)
    chv[:, 128:256] = jnp.max(jnp.where(where == lane + 128, block, 0), axis=0, keepdims=True)
    choose = pltpu.make_async_copy(chv, chs, lsem.at[5])
    choose.start()
    choose.wait()

    for i in (12, 13, 14, 15):
        c[i].wait_recv()
    loads[1].wait()

    def widen(s, carry):
        rows = cbuf[s // SIDE, lax.rem(s, SIDE)].astype(jnp.float32)
        for j in range(NBLK):
            cf[s * NBLK + j] = rows[j * BLK : (j + 1) * BLK]
        return carry

    lax.fori_loop(0, CHIPS, widen, 0)

    two = 2 * WORK // BLK

    def input_grad(s, carry):
        for j in range(two):
            b = chs[0, s * two + j]
            stage[pl.ds(j * BLK, BLK), :] = cf[b]
        rows = lax.dot_general(
            stage[...].astype(jnp.bfloat16), w[...], (((1,), (1,)), ((), ())),
            preferred_element_type=jnp.float32,
        )
        gbuf[pl.ds(2 * s, 2)] = rows.astype(jnp.bfloat16).reshape(2, WORK, COLS)
        return carry

    lax.fori_loop(0, CHIPS // 2, input_grad, 0)

    def owners(dx, dy):
        to = plane(dx, dy)
        i = dy * SIDE + dx
        return remote(
            gbuf.at[to], ig_out.at[:, pl.ds(pl.multiple_of(chip * COLS, 128), COLS)],
            gsend.at[i], grecv.at[i], node, to,
        )

    loads[4].wait()

    def contract(dy, cols):
        s = lax.rem(y + SIDE - dy, SIDE)
        part = lax.dot_general(
            xr[pl.ds(s * SIDE, SIDE)].reshape(SIDE * SLOT, COLS),
            cbuf[s, :, :, cols].reshape(SIDE * SLOT, cols.stop - cols.start),
            (((0,), (0,)), ((), ())), preferred_element_type=jnp.float32,
        )
        if dy == 0:
            acc[:, cols] = part
        else:
            acc[:, cols] += part

    def arrived(dy):
        for dx in range(SIDE):
            if (dx, dy) != (0, 0):
                xs[dx, dy].wait_recv()

    for dy in (0, 1, 3):
        arrived(dy)
        contract(dy, slice(0, KV))

    own_grad = pltpu.make_async_copy(
        gbuf.at[chip], ig_out.at[:, pl.ds(pl.multiple_of(chip * COLS, 128), COLS)], lsem.at[6]
    )
    own_grad.start()
    for o in ALL:
        xs[o].wait_send()
    gs = [owners(*o) for o in ALL]
    for g in gs:
        g.start()

    def compress(which, h):
        def one(k, carry):
            p = pl.multiple_of((k * 2 + which) * PIECE, PIECE)
            cols = slice(h * HALF, (h + 1) * HALF)
            e = acc[pl.ds(p, PIECE), cols] + serr[pl.ds(p, PIECE), cols].astype(jnp.float32)
            sent, left = squash(e)
            for j in range(HALF // 128):
                sbuf[h, which, k, :, 128 * j : 128 * (j + 1)] = sent[j]
                at = h * HALF + 128 * j
                nse_out[pl.ds(p, PIECE), at : at + 128] = left[j].astype(jnp.bfloat16)
            return carry

        lax.fori_loop(0, DEPTH, one, 0)

    loads[2].wait()
    loads[3].wait()
    arrived(2)
    pair, zc = [], [{}, {}]
    for h in (0, 1):
        contract(2, slice(h * HALF, (h + 1) * HALF))
        compress(other, h)
        pair.append(remote(sbuf.at[h, other], sib.at[h], ssend.at[h], srecv.at[h], z * 2 + other, chip))
        pair[h].start()
        compress(core, h)
        pair[h].wait_recv()
        for dz in Z_ORDER:
            to = deep(dz)
            zs[h, to] = (
                sbuf[h, core, to].astype(jnp.float32) + sib[h, to].astype(jnp.float32)
            ).astype(jnp.bfloat16)
            zc[h][dz] = remote(
                zs.at[h, to], zr.at[h, dz], zsend.at[h, dz], zrecv.at[h, dz], to * 2 + core, chip
            )
            zc[h][dz].start()

    sent_on = []

    def ring(h, step, up):
        n = deep(DEPTH - step if up else step) * 2 + core
        cols = pl.ds(h * HALF, HALF)
        if step == 3:
            cols = pl.ds(h * HALF + (0 if up else HALF // 2), HALF // 2)
        i = (h * 4 + step) * 2 + (1 if up else 0)
        return remote(
            upd_out.at[n, :, cols], upd_out.at[n, :, cols], usend.at[i], urecv.at[i],
            deep(1 if up else DEPTH - 1) * 2 + core, chip,
        )

    def share(h, dz):
        n = deep(dz) * 2 + core
        block = upd_out.at[n, :, pl.ds(h * HALF, HALF)]
        i = h * DEPTH + dz
        f = remote(block, block, fsend.at[i], frecv.at[i], z * 2 + other, chip)
        f.start()
        return f

    us, fs = {}, []

    def average(h):
        cols = slice(h * HALF, (h + 1) * HALF)
        total = sbuf[h, core, z].astype(jnp.float32) + sib[h, z].astype(jnp.float32)
        for dz in reversed(Z_ORDER):
            zc[h][dz].wait_recv()
            total = total + zr[h, dz].astype(jnp.float32)
        sent, left = squash(total * (1.0 / 16) + merr[:, cols])
        for j in range(HALF // 128):
            at = h * HALF + 128 * j
            upd_out[node, :, at : at + 128] = sent[j]
            nme_out[:, at : at + 128] = left[j]
        forward(h, 0)
        fs.append(share(h, 0))

    def forward(h, step):
        for up in (True, False):
            if step:
                us[h, step - 1, up].wait_recv()
            if step < 4:
                us[h, step, up] = ring(h, step, up)
                us[h, step, up].start()
        if step in (1, 2, 3):
            fs.append(share(h, DEPTH - step))
            fs.append(share(h, step))
        elif step == 4:
            fs.append(share(h, 4))

    average(0)
    forward(0, 1)
    average(1)
    for step in (2, 3, 4):
        forward(0, step)
        forward(1, step - 1)
    forward(1, 4)
    for f in fs:
        f.wait_recv()
    own_grad.wait()
    for g in gs:
        g.wait_recv()
    for s in c + ps + gs + fs + pair + list(zc[0].values()) + list(zc[1].values()) + list(us.values()):
        s.wait_send()


def leave(ig, nse, nme, upd, ig_out, nse_out, nme_out, upd_out, ig_v, nse_v, nme_v, upd_v, get, put):
    parts = []
    for src, mid, dst in ((ig, ig_v, ig_out), (nse, nse_v, nse_out), (upd, upd_v, upd_out), (nme, nme_v, nme_out)):
        step = min(src.shape[0], 2 * PIECE)
        for r in range(0, src.shape[0], step):
            n = min(step, src.shape[0] - r)
            parts.append([ref.at[pl.ds(r, n)] for ref in (src, mid, dst)])
    reads = [pltpu.make_async_copy(a, b, get.at[i]) for i, (a, b, _) in enumerate(parts)]
    writes = [pltpu.make_async_copy(b, c, put.at[i]) for i, (_, b, c) in enumerate(parts)]
    for read in reads:
        read.start()
    for read, write in zip(reads, writes):
        read.wait()
        write.start()
    for write in writes:
        write.wait()


def per_device(
    x_rows, value_cot, value_weight, resp_of_row, block_plan, resp_len, group_of_resp, rewards, send_error, mean_error
):
    vmem = pl.BlockSpec(memory_space=pltpu.VMEM)
    hbm = pl.BlockSpec(memory_space=pl.ANY)
    bf16, f32, i32 = jnp.bfloat16, jnp.float32, jnp.int32
    dma = pltpu.SemaphoreType.DMA
    ig, nse, nme, upd = pl.pallas_call(
        kernel,
        out_shape=(
            jax.ShapeDtypeStruct((WORK, CHIPS * COLS), bf16),
            jax.ShapeDtypeStruct((COLS, KV), bf16),
            jax.ShapeDtypeStruct((PIECE, KV), f32),
            jax.ShapeDtypeStruct((CHIPS, PIECE, KV), bf16),
        ),
        in_specs=[hbm, hbm, hbm, vmem, vmem, vmem, vmem, vmem, hbm, hbm],
        out_specs=(hbm, vmem, vmem, vmem),
        scratch_shapes=[
            pltpu.VMEM((SLOT, KV), bf16),
            pltpu.VMEM((COLS, KV), bf16),
            pltpu.VMEM((COLS, KV), bf16),
            pltpu.VMEM((PIECE, KV), f32),
            pltpu.VMEM((SIDE, SIDE, SLOT, KV), bf16),
            pltpu.VMEM((CHIPS * NBLK, BLK, KV), f32),
            pltpu.VMEM((CHIPS, SLOT, COLS), bf16),
            pltpu.VMEM((2 * WORK, KV), f32),
            pltpu.VMEM((CHIPS, WORK, COLS), bf16),
            pltpu.VMEM((COLS, KV), f32),
            pltpu.VMEM((2, 2, DEPTH, PIECE, HALF), bf16),
            pltpu.VMEM((2, DEPTH, PIECE, HALF), bf16),
            pltpu.VMEM((2, DEPTH, PIECE, HALF), bf16),
            pltpu.VMEM((2, DEPTH, PIECE, HALF), bf16),
            pltpu.VMEM((CHIPS, NBLK, 128), i32),
            pltpu.VMEM((1, 256), i32),
            pltpu.SMEM((1, 256), i32),
            dma((8,)), dma((16,)), dma((16,)), dma((16,)), dma((16,)), dma((16,)), dma((16,)),
            dma((16,)), dma((16,)), dma((2,)), dma((2,)), dma((2, 8)), dma((2, 8)), dma((16,)), dma((16,)),
            dma((16,)), dma((16,)),
        ],
        compiler_params=pltpu.CompilerParams(
            collective_id=0, has_side_effects=True, vmem_limit_bytes=58 * 2**20
        ),
        cost_estimate=pl.CostEstimate(flops=8_000_000_000, bytes_accessed=20_000_000, transcendentals=800_000),
    )(
        x_rows, value_cot, value_weight, resp_of_row.reshape(1, SLOT), block_plan.T,
        resp_len.reshape(1, -1), group_of_resp.reshape(1, -1), rewards.reshape(1, -1),
        send_error.reshape(COLS, KV), mean_error.reshape(PIECE, KV),
    )
    upd = upd.reshape(COLS, KV)
    ig, nse, nme, upd = pl.pallas_call(
        leave,
        out_shape=tuple(jax.ShapeDtypeStruct(a.shape, a.dtype) for a in (ig, nse, nme, upd)),
        in_specs=[hbm] * 4,
        out_specs=[hbm] * 4,
        scratch_shapes=[pltpu.VMEM(a.shape, a.dtype) for a in (ig, nse, nme, upd)] + [dma((24,)), dma((24,))],
        compiler_params=pltpu.CompilerParams(vmem_limit_bytes=58 * 2**20),
    )(ig, nse, nme, upd)
    return ig, nse[None], nme[None, None], upd


def solution(mesh):
    return jax.shard_map(
        per_device,
        mesh=mesh,
        in_specs=(
            P(("node", "chip"), None),
            P(("node", "chip"), None),
            P("chip", None),
            P(("node", "chip")),
            P(("node", "chip"), None),
            P(),
            P(),
            P(),
            P("node", "chip", None),
            P("chip", "node", None, None),
        ),
        out_specs=(
            P(("node", "chip"), None),
            P("node", "chip", None),
            P("chip", "node", None, None),
            P("chip", None),
        ),
        check_vma=False,
    )
```

```python
import functools

import jax
import jax.numpy as jnp
from jax import lax
from jax.experimental import pallas as pl
from jax.experimental.pallas import tpu as pltpu
from jax.sharding import PartitionSpec as P

MESH = pl.DeviceIdType.MESH
GSIZE = 8
SIDE = 4
CHIPS = 16
BLK = 12
NBLK = 16
SLOT = 192
WORK = 144
KV = 1024
COLS = 768
PIECE = 48
DEPTH = 8
HALF = KV // 2

GROUPS = (
    ((1, 0), (3, 0), (0, 1), (0, 3)),
    ((2, 0), (0, 2)),
    ((1, 1), (3, 3)),
    ((1, 3), (3, 1)),
    ((2, 1), (2, 3)),
    ((2, 2),),
    ((1, 2), (3, 2)),
)
ALL = tuple(o for group in GROUPS for o in group)
Z_ORDER = (4, 3, 5, 2, 6, 1, 7)


def squash(e):
    sent, left = [], []
    for j in range(e.shape[1] // 128):
        g = e[:, 128 * j : 128 * (j + 1)]
        m = jnp.mean(jnp.abs(g), axis=1, keepdims=True) + 1e-06
        s = (m * jnp.tanh(g * (1.0 / m))).astype(jnp.bfloat16)
        sent.append(s)
        left.append(g - s.astype(jnp.float32))
    return sent, left


def upright(row):
    n = row.shape[1]
    here = lax.broadcasted_iota(jnp.int32, (n, n), 0) == lax.broadcasted_iota(jnp.int32, (n, n), 1)
    return jnp.sum(jnp.where(here, row, 0), axis=1, keepdims=True)


def row_weights(resp, rlen, grp, rew):
    resp_total = rew.shape[1]
    groups = resp_total // GSIZE
    member = lax.broadcasted_iota(jnp.int32, (groups, resp_total), 0) == grp
    mean = jnp.sum(jnp.where(member, rew, 0.0), axis=1, keepdims=True) / GSIZE
    advantage = rew - jnp.sum(jnp.where(member, mean, 0.0), axis=0, keepdims=True)
    lookup = advantage / rlen.astype(jnp.float32)
    ids = lax.broadcasted_iota(jnp.int32, (SLOT, resp_total), 1)
    return jnp.sum(jnp.where(resp == ids, lookup, 0.0), axis=1, keepdims=True)


def kernel(
    x_hbm, cot_hbm, w_hbm, resp_ref, plan_ref, rlen_ref, grp_ref, rew_ref, serr_hbm, merr_hbm,
    ig_out, nse_out, nme_out, upd_out,
    cot, w, serr, merr, cbuf, cf, xr, stage, gbuf, acc, sbuf, sib, zs, zr, pbuf, chv, chs,
    lsem, csend, crecv, xsend, xrecv, psend, precv, gsend, grecv,
    ssend, srecv, zsend, zrecv, usend, urecv, fsend, frecv,
):
    node, chip = lax.axis_index("node"), lax.axis_index("chip")
    y, x = chip // SIDE, lax.rem(chip, SIDE)
    z, core = node // 2, lax.rem(node, 2)
    other = 1 - core

    def plane(dx, dy):
        return lax.rem(y + dy, SIDE) * SIDE + lax.rem(x + dx, SIDE)

    def deep(dz):
        return lax.rem(z + dz, DEPTH)

    def remote(src, dst, send, recv, node_to, chip_to):
        return pltpu.make_async_remote_copy(
            src_ref=src, dst_ref=dst, send_sem=send, recv_sem=recv,
            device_id=(node_to, chip_to), device_id_type=MESH,
        )

    barrier = pltpu.get_barrier_semaphore()
    for dx, dy in ALL:
        pl.semaphore_signal(barrier, 1, device_id=(node, plane(dx, dy)), device_id_type=MESH)
    for dz in Z_ORDER:
        pl.semaphore_signal(barrier, 1, device_id=(deep(dz) * 2 + core, chip), device_id_type=MESH)
    pl.semaphore_signal(barrier, 1, device_id=(z * 2 + other, chip), device_id_type=MESH)

    loads = [
        pltpu.make_async_copy(cot_hbm, cot, lsem.at[0]),
        pltpu.make_async_copy(w_hbm, w, lsem.at[1]),
        pltpu.make_async_copy(serr_hbm, serr, lsem.at[2]),
        pltpu.make_async_copy(merr_hbm, merr, lsem.at[3]),
        pltpu.make_async_copy(
            x_hbm.at[:, pl.ds(pl.multiple_of(chip * COLS, 128), COLS)], xr.at[chip], lsem.at[4]
        ),
    ]
    for load in loads:
        load.start()

    weight = row_weights(upright(resp_ref[...]), rlen_ref[...], grp_ref[...], rew_ref[...])
    goes = plan_ref[...]
    target = jnp.where(goes[0:1] >= 0, goes[0:1] * (WORK // BLK) + goes[2:3], -1)
    pbuf[chip] = jnp.broadcast_to(upright(target), (NBLK, 128))
    loads[0].wait()
    cbuf[y, x] = (weight * cot[...].astype(jnp.float32)).astype(jnp.bfloat16)

    pl.semaphore_wait(barrier, len(ALL) + len(Z_ORDER) + 1)

    xp, xm = lax.rem(x + 1, SIDE), lax.rem(x + 3, SIDE)
    yp, ym = lax.rem(y + 1, SIDE), lax.rem(y + 3, SIDE)
    half, quarter = SLOT // 2, SLOT // 4

    def hop(i, block, to_y, to_x):
        return remote(block, block, csend.at[i], crecv.at[i], node, to_y * SIDE + to_x)

    lo, hi = pl.ds(0, half), pl.ds(half, half)
    q0, q1, q2, q3 = (pl.ds(quarter * i, quarter) for i in range(4))
    c = [
        hop(0, cbuf.at[y, x, lo], y, xp),
        hop(1, cbuf.at[y, x, lo], y, xm),
        hop(2, cbuf.at[y, x, hi], yp, x),
        hop(3, cbuf.at[y, x, hi], ym, x),
        hop(4, cbuf.at[y, xm, q0], y, xp),
        hop(5, cbuf.at[y, xp, q1], y, xm),
        hop(6, cbuf.at[ym, x, q2], yp, x),
        hop(7, cbuf.at[yp, x, q3], ym, x),
        hop(8, cbuf.at[y, :, lo], yp, x),
        hop(9, cbuf.at[y, :, lo], ym, x),
        hop(10, cbuf.at[:, x, hi], y, xp),
        hop(11, cbuf.at[:, x, hi], y, xm),
        hop(12, cbuf.at[ym, :, q0], yp, x),
        hop(13, cbuf.at[yp, :, q1], ym, x),
        hop(14, cbuf.at[:, xm, q2], y, xp),
        hop(15, cbuf.at[:, xp, q3], y, xm),
    ]

    def columns(dx, dy):
        to = plane(dx, dy)
        i = dy * SIDE + dx
        return remote(
            x_hbm.at[:, pl.ds(pl.multiple_of(to * COLS, 128), COLS)], xr.at[chip],
            xsend.at[i], xrecv.at[i], node, to,
        )

    def plans(dx, dy):
        i = dy * SIDE + dx
        return remote(pbuf.at[chip], pbuf.at[chip], psend.at[i], precv.at[i], node, plane(dx, dy))

    xs = {o: columns(*o) for o in ALL}
    ps = [plans(*o) for o in ALL]

    for i in (0, 1, 2, 3):
        c[i].start()
    for p in ps:
        p.start()
    for o in GROUPS[0] + GROUPS[1] + GROUPS[2] + GROUPS[3]:
        xs[o].start()
    for i in (0, 1, 2, 3):
        c[i].wait_recv()
        c[i + 4].start()
    for i in (4, 5):
        c[i].wait_recv()
    c[8].start()
    c[9].start()
    for i in (6, 7):
        c[i].wait_recv()
    c[10].start()
    c[11].start()
    for o in GROUPS[4] + GROUPS[5]:
        xs[o].start()
    for i in (8, 9, 10, 11):
        c[i].wait_recv()
        c[i + 4].start()
    for o in GROUPS[6]:
        xs[o].start()

    for p in ps:
        p.wait_recv()
    where = pbuf[...].reshape(CHIPS * NBLK, 128)
    block = lax.broadcasted_iota(jnp.int32, (CHIPS * NBLK, 128), 0)
    lane = lax.broadcasted_iota(jnp.int32, (CHIPS * NBLK, 128), 1)
    chv[:, 0:128] = jnp.max(jnp.where(where == lane, block, 0), axis=0, keepdims=True)
    chv[:, 128:256] = jnp.max(jnp.where(where == lane + 128, block, 0), axis=0, keepdims=True)
    choose = pltpu.make_async_copy(chv, chs, lsem.at[5])
    choose.start()
    choose.wait()

    for i in (12, 13, 14, 15):
        c[i].wait_recv()
    loads[1].wait()

    def widen(s, carry):
        rows = cbuf[s // SIDE, lax.rem(s, SIDE)].astype(jnp.float32)
        for j in range(NBLK):
            cf[s * NBLK + j] = rows[j * BLK : (j + 1) * BLK]
        return carry

    lax.fori_loop(0, CHIPS, widen, 0)

    two = 2 * WORK // BLK

    def input_grad(s, carry):
        for j in range(two):
            b = chs[0, s * two + j]
            stage[pl.ds(j * BLK, BLK), :] = cf[b]
        rows = lax.dot_general(
            stage[...].astype(jnp.bfloat16), w[...], (((1,), (1,)), ((), ())),
            preferred_element_type=jnp.float32,
        )
        gbuf[pl.ds(2 * s, 2)] = rows.astype(jnp.bfloat16).reshape(2, WORK, COLS)
        return carry

    lax.fori_loop(0, CHIPS // 2, input_grad, 0)

    def owners(dx, dy):
        to = plane(dx, dy)
        i = dy * SIDE + dx
        return remote(
            gbuf.at[to], ig_out.at[:, pl.ds(pl.multiple_of(chip * COLS, 128), COLS)],
            gsend.at[i], grecv.at[i], node, to,
        )

    loads[4].wait()

    def contract(dy, cols):
        s = lax.rem(y + SIDE - dy, SIDE)
        part = lax.dot_general(
            xr[pl.ds(s * SIDE, SIDE)].reshape(SIDE * SLOT, COLS),
            cbuf[s, :, :, cols].reshape(SIDE * SLOT, cols.stop - cols.start),
            (((0,), (0,)), ((), ())), preferred_element_type=jnp.float32,
        )
        if dy == 0:
            acc[:, cols] = part
        else:
            acc[:, cols] += part

    def arrived(dy):
        for dx in range(SIDE):
            if (dx, dy) != (0, 0):
                xs[dx, dy].wait_recv()

    for dy in (0, 1, 3):
        arrived(dy)
        contract(dy, slice(0, KV))

    own_grad = pltpu.make_async_copy(
        gbuf.at[chip], ig_out.at[:, pl.ds(pl.multiple_of(chip * COLS, 128), COLS)], lsem.at[6]
    )
    own_grad.start()
    for o in ALL:
        xs[o].wait_send()
    gs = [owners(*o) for o in ALL]
    for g in gs:
        g.start()

    def compress(which, h):
        def one(k, carry):
            p = pl.multiple_of((k * 2 + which) * PIECE, PIECE)
            cols = slice(h * HALF, (h + 1) * HALF)
            e = acc[pl.ds(p, PIECE), cols] + serr[pl.ds(p, PIECE), cols].astype(jnp.float32)
            sent, left = squash(e)
            for j in range(HALF // 128):
                sbuf[h, which, k, :, 128 * j : 128 * (j + 1)] = sent[j]
                at = h * HALF + 128 * j
                nse_out[pl.ds(p, PIECE), at : at + 128] = left[j].astype(jnp.bfloat16)
            return carry

        lax.fori_loop(0, DEPTH, one, 0)

    loads[2].wait()
    loads[3].wait()
    arrived(2)
    pair, zc = [], [{}, {}]
    for h in (0, 1):
        contract(2, slice(h * HALF, (h + 1) * HALF))
        compress(other, h)
        pair.append(remote(sbuf.at[h, other], sib.at[h], ssend.at[h], srecv.at[h], z * 2 + other, chip))
        pair[h].start()
        compress(core, h)
        pair[h].wait_recv()
        for dz in Z_ORDER:
            to = deep(dz)
            zs[h, to] = (
                sbuf[h, core, to].astype(jnp.float32) + sib[h, to].astype(jnp.float32)
            ).astype(jnp.bfloat16)
            zc[h][dz] = remote(
                zs.at[h, to], zr.at[h, dz], zsend.at[h, dz], zrecv.at[h, dz], to * 2 + core, chip
            )
            zc[h][dz].start()

    sent_on = []

    def ring(h, step, up):
        n = deep(DEPTH - step if up else step) * 2 + core
        cols = pl.ds(h * HALF, HALF)
        if step == 3:
            cols = pl.ds(h * HALF + (0 if up else HALF // 2), HALF // 2)
        i = (h * 4 + step) * 2 + (1 if up else 0)
        return remote(
            upd_out.at[n, :, cols], upd_out.at[n, :, cols], usend.at[i], urecv.at[i],
            deep(1 if up else DEPTH - 1) * 2 + core, chip,
        )

    def share(h, dz):
        n = deep(dz) * 2 + core
        block = upd_out.at[n, :, pl.ds(h * HALF, HALF)]
        i = h * DEPTH + dz
        f = remote(block, block, fsend.at[i], frecv.at[i], z * 2 + other, chip)
        f.start()
        return f

    us, fs = {}, []

    def average(h):
        cols = slice(h * HALF, (h + 1) * HALF)
        total = sbuf[h, core, z].astype(jnp.float32) + sib[h, z].astype(jnp.float32)
        for dz in reversed(Z_ORDER):
            zc[h][dz].wait_recv()
            total = total + zr[h, dz].astype(jnp.float32)
        sent, left = squash(total * (1.0 / 16) + merr[:, cols])
        for j in range(HALF // 128):
            at = h * HALF + 128 * j
            upd_out[node, :, at : at + 128] = sent[j]
            nme_out[:, at : at + 128] = left[j]
        forward(h, 0)
        fs.append(share(h, 0))

    def forward(h, step):
        for up in (True, False):
            if step:
                us[h, step - 1, up].wait_recv()
            if step < 4:
                us[h, step, up] = ring(h, step, up)
                us[h, step, up].start()
        if step in (1, 2, 3):
            fs.append(share(h, DEPTH - step))
            fs.append(share(h, step))
        elif step == 4:
            fs.append(share(h, 4))

    average(0)
    forward(0, 1)
    average(1)
    for step in (2, 3, 4):
        forward(0, step)
        forward(1, step - 1)
    forward(1, 4)
    for f in fs:
        f.wait_recv()
    own_grad.wait()
    for g in gs:
        g.wait_recv()
    for s in c + ps + gs + fs + pair + list(zc[0].values()) + list(zc[1].values()) + list(us.values()):
        s.wait_send()


def leave(ig, nse, nme, upd, ig_out, nse_out, nme_out, upd_out, ig_v, nse_v, nme_v, upd_v, get, put):
    parts = []
    for src, mid, dst in ((ig, ig_v, ig_out), (nse, nse_v, nse_out), (upd, upd_v, upd_out), (nme, nme_v, nme_out)):
        step = min(src.shape[0], 2 * PIECE)
        for r in range(0, src.shape[0], step):
            n = min(step, src.shape[0] - r)
            parts.append([ref.at[pl.ds(r, n)] for ref in (src, mid, dst)])
    reads = [pltpu.make_async_copy(a, b, get.at[i]) for i, (a, b, _) in enumerate(parts)]
    writes = [pltpu.make_async_copy(b, c, put.at[i]) for i, (_, b, c) in enumerate(parts)]
    for read in reads:
        read.start()
    for read, write in zip(reads, writes):
        read.wait()
        write.start()
    for write in writes:
        write.wait()


def per_device(
    x_rows, value_cot, value_weight, resp_of_row, block_plan, resp_len, group_of_resp, rewards, send_error, mean_error
):
    vmem = pl.BlockSpec(memory_space=pltpu.VMEM)
    hbm = pl.BlockSpec(memory_space=pl.ANY)
    bf16, f32, i32 = jnp.bfloat16, jnp.float32, jnp.int32
    dma = pltpu.SemaphoreType.DMA
    ig, nse, nme, upd = pl.pallas_call(
        kernel,
        out_shape=(
            jax.ShapeDtypeStruct((WORK, CHIPS * COLS), bf16),
            jax.ShapeDtypeStruct((COLS, KV), bf16),
            jax.ShapeDtypeStruct((PIECE, KV), f32),
            jax.ShapeDtypeStruct((CHIPS, PIECE, KV), bf16),
        ),
        in_specs=[hbm, hbm, hbm, vmem, vmem, vmem, vmem, vmem, hbm, hbm],
        out_specs=(hbm, vmem, vmem, vmem),
        scratch_shapes=[
            pltpu.VMEM((SLOT, KV), bf16),
            pltpu.VMEM((COLS, KV), bf16),
            pltpu.VMEM((COLS, KV), bf16),
            pltpu.VMEM((PIECE, KV), f32),
            pltpu.VMEM((SIDE, SIDE, SLOT, KV), bf16),
            pltpu.VMEM((CHIPS * NBLK, BLK, KV), f32),
            pltpu.VMEM((CHIPS, SLOT, COLS), bf16),
            pltpu.VMEM((2 * WORK, KV), f32),
            pltpu.VMEM((CHIPS, WORK, COLS), bf16),
            pltpu.VMEM((COLS, KV), f32),
            pltpu.VMEM((2, 2, DEPTH, PIECE, HALF), bf16),
            pltpu.VMEM((2, DEPTH, PIECE, HALF), bf16),
            pltpu.VMEM((2, DEPTH, PIECE, HALF), bf16),
            pltpu.VMEM((2, DEPTH, PIECE, HALF), bf16),
            pltpu.VMEM((CHIPS, NBLK, 128), i32),
            pltpu.VMEM((1, 256), i32),
            pltpu.SMEM((1, 256), i32),
            dma((8,)), dma((16,)), dma((16,)), dma((16,)), dma((16,)), dma((16,)), dma((16,)),
            dma((16,)), dma((16,)), dma((2,)), dma((2,)), dma((2, 8)), dma((2, 8)), dma((16,)), dma((16,)),
            dma((16,)), dma((16,)),
        ],
        compiler_params=pltpu.CompilerParams(
            collective_id=0, has_side_effects=True, vmem_limit_bytes=58 * 2**20
        ),
        cost_estimate=pl.CostEstimate(flops=8_000_000_000, bytes_accessed=20_000_000, transcendentals=800_000),
    )(
        x_rows, value_cot, value_weight, resp_of_row.reshape(1, SLOT), block_plan.T,
        resp_len.reshape(1, -1), group_of_resp.reshape(1, -1), rewards.reshape(1, -1),
        send_error.reshape(COLS, KV), mean_error.reshape(PIECE, KV),
    )
    upd = upd.reshape(COLS, KV)
    ig, nse, nme, upd = pl.pallas_call(
        leave,
        out_shape=tuple(jax.ShapeDtypeStruct(a.shape, a.dtype) for a in (ig, nse, nme, upd)),
        in_specs=[hbm] * 4,
        out_specs=[hbm] * 4,
        scratch_shapes=[pltpu.VMEM(a.shape, a.dtype) for a in (ig, nse, nme, upd)] + [dma((24,)), dma((24,))],
        compiler_params=pltpu.CompilerParams(vmem_limit_bytes=58 * 2**20),
    )(ig, nse, nme, upd)
    return ig, nse[None], nme[None, None], upd


def solution(mesh):
    return jax.shard_map(
        per_device,
        mesh=mesh,
        in_specs=(
            P(("node", "chip"), None),
            P(("node", "chip"), None),
            P("chip", None),
            P(("node", "chip")),
            P(("node", "chip"), None),
            P(),
            P(),
            P(),
            P("node", "chip", None),
            P("chip", "node", None, None),
        ),
        out_specs=(
            P(("node", "chip"), None),
            P("node", "chip", None),
            P("chip", "node", None, None),
            P("chip", None),
        ),
        check_vma=False,
    )
```
